256 devices in a mesh: tm: 16 (over x_lo, z), space: 16 (over x_hi, y, core).
Axes of the slice: x: 4 (x_hi: 2, x_lo: 2; x = x_hi * 2 + x_lo), y: 4, z: 8, core: 2. Of those that a mesh axis runs over, the one named last changes fastest.
Arguments:
- latent: bfloat16 [2, 16, 2048, 1152], P(None, 'tm', 'space'), may hold values from -6 to 6
- spatial_cache: bfloat16 [2, 16, 2048, 1152], P(None, 'tm', 'space'), may hold values from -6 to 6
- modulation: float32 [2, 2, 3, 1152], replicated, may hold values from -3 to 3
- weights: bfloat16 [2, 1152, 4608], P(None, 'tm'), may hold values from -0.1875 to 0.1875
Outputs:
- block_out: bfloat16 [2, 16, 2048, 1152], P(None, 'tm', 'space')
- new_spatial: bfloat16 [2, 16, 2048, 1152], P(None, 'tm', 'space')
- new_temporal: bfloat16 [2, 16, 2048, 1152], P(None, 'tm', 'space')
The draws below stay inside these ranges and needn't reach their ends.
All inputs are finite; a program needn't handle non-finite values.
Results may differ from the reference program's by a relative error of at most 0.015.
Values may be sent and summed in bfloat16 or wider, within the bound.
No kernel may reach another device: no remote copies, remote signals or barrier semaphores. Data moves between devices by JAX's collectives and lax.ppermute only.
A program may use at most 128 MiB of HBM per device.

```python
import jax
import jax.numpy as jnp
from jax import lax

D = 1152
HEADS = 16
HEAD_DIM = 72
BATCH = 2
FRAMES = 16
SPAN = 2048


def levels(key, dims, split, least, largest):
    factor_of, own = 1.0, jax.random.fold_in(key, 6)
    for dim, blocks in split:
        steps = jnp.exp(jax.random.uniform(jax.random.fold_in(own, dim), (blocks,), jnp.float32, least / len(split), largest / len(split)))
        factor_of = factor_of * jnp.repeat(steps, dims[dim] // blocks).reshape([-1 if axis == dim else 1 for axis in range(len(dims))])
    return factor_of


def gaussian(own_key, shape, width, limit, pieces=(), kind=jnp.bfloat16):
    result = jax.random.normal(own_key, shape, jnp.float32) * width
    if len(pieces) > 0:
        result = levels(own_key, shape, pieces, -0.22, 0.18) * result
    return jnp.clip(result, min=-limit, max=limit).astype(kind)


def setup_inputs(seed: int = 0) -> dict:
    streams_of = jax.random.split(jax.random.key(seed), 5)
    latent = gaussian(streams_of[0], (BATCH, FRAMES, SPAN, D), 1.0, 6.0, ((1, 16), (2, 16)))
    spatial_cache = gaussian(streams_of[1], (BATCH, FRAMES, SPAN, D), 1.0, 6.0, ((1, 16), (2, 16)))
    modulation = gaussian(streams_of[2], (2, 2, 3, D), 0.5, 3.0, (), jnp.float32)
    weights = gaussian(streams_of[3], (2, D, 4 * D), D ** -0.5, 0.1875, ((1, 16),))
    return dict(latent=latent, spatial_cache=spatial_cache, modulation=modulation, weights=weights)


def layer_norm(h):
    x = h.astype(jnp.float32)
    mean = lax.optimization_barrier(jnp.mean(x, axis=-1, keepdims=True))
    var = lax.optimization_barrier(jnp.mean((x - mean) ** 2, axis=-1, keepdims=True))
    return (x - mean) * lax.rsqrt(var + 1e-06)

def modulate(h, mods):
    return (layer_norm(h) * (1.0 + mods[1]) + mods[0]).astype(jnp.bfloat16)

def rms_norm(v):
    return v * lax.rsqrt(lax.optimization_barrier(jnp.mean(v * v, axis=-1, keepdims=True)) + 1e-06)

def attend(query, keys, values):
    scores = jnp.einsum('nlhd,nmhd->nhlm', query.astype(jnp.float32), keys.astype(jnp.float32)) / jnp.sqrt(jnp.float32(HEAD_DIM))
    expo = jnp.exp(scores)
    probs = (expo / lax.optimization_barrier(jnp.sum(expo, axis=-1, keepdims=True))).astype(jnp.bfloat16)
    out = jnp.einsum('nhlm,nmhd->nlhd', probs.astype(jnp.float32), values.astype(jnp.float32))
    return out.astype(jnp.bfloat16)

def fresh_attention(h, mods, weight, spatial):
    modin = modulate(h, mods)
    flat = modin.reshape(-1, D)
    qkv = jnp.dot(flat, weight[:, :3 * D], preferred_element_type=jnp.float32)
    qkv = qkv.reshape(BATCH, FRAMES, SPAN, HEADS, 3, HEAD_DIM)
    query = rms_norm(qkv[..., 0, :]).astype(jnp.bfloat16)
    keys = rms_norm(qkv[..., 1, :]).astype(jnp.bfloat16)
    values = qkv[..., 2, :].astype(jnp.bfloat16)
    if spatial:
        shape = (BATCH * FRAMES, 1, SPAN, HEADS, HEAD_DIM)
        items = (query.reshape(shape), keys.reshape(shape), values.reshape(shape))
        out = lax.map(lambda t: attend(t[0], t[1], t[2]), items)
        out = out.reshape(BATCH, FRAMES, SPAN, D)
    else:

        def tokens_major(t):
            return jnp.transpose(t, (0, 2, 1, 3, 4)).reshape(BATCH * SPAN, FRAMES, HEADS, HEAD_DIM)
        out = attend(tokens_major(query), tokens_major(keys), tokens_major(values))
        out = jnp.transpose(out.reshape(BATCH, SPAN, FRAMES, D), (0, 2, 1, 3))
    proj = jnp.dot(out.reshape(-1, D), weight[:, 3 * D:], preferred_element_type=jnp.float32)
    return proj.astype(jnp.bfloat16).reshape(BATCH, FRAMES, SPAN, D)

def add_gated(h, gate, branch):
    return (h.astype(jnp.float32) + gate * branch.astype(jnp.float32)).astype(jnp.bfloat16)

def reference(latent, spatial_cache, modulation, weights):
    h = add_gated(latent, modulation[0, 0, 2], spatial_cache)
    new_temporal = fresh_attention(h, modulation[0, 1], weights[1], False)
    h = add_gated(h, modulation[0, 1, 2], new_temporal)
    new_spatial = fresh_attention(h, modulation[1, 0], weights[0], True)
    h = add_gated(h, modulation[1, 0, 2], new_spatial)
    block_out = add_gated(h, modulation[1, 1, 2], new_temporal)
    return (block_out, new_spatial, new_temporal)
```

```python
import math

import jax
import jax.numpy as jnp
from jax import lax
from jax.experimental import pallas as pl
from jax.experimental.pallas import tpu as pltpu
from jax.sharding import Mesh, PartitionSpec as P

D = 1152
HD = 72
HALF = D // 2
QKV = 3 * HALF
TOK = 256
SCALE = math.log2(math.e) / math.sqrt(HD)
TM = ("xl", "z")
SPACE = ("xh", "y", "c")
XX = ("xl", "xh")
BF = jnp.bfloat16
F32 = jnp.float32
VMEM = pl.BlockSpec(memory_space=pltpu.VMEM)
SMEM = pl.BlockSpec(memory_space=pltpu.SMEM)


def x_pairs(step):
    place = lambda x: (x % 2) * 2 + x // 2
    return [(place(x), place((x + step) % 4)) for x in range(4)]


CORE = [(0, 1), (1, 0)]
X_UP, X_DOWN = x_pairs(1), x_pairs(-1)


def call(body, name, outs, ins, scratch=(), flops=0, nbytes=0, trans=0):
    return pl.pallas_call(
        body,
        name=name,
        out_shape=outs,
        in_specs=ins,
        out_specs=jax.tree.map(lambda _: VMEM, outs),
        scratch_shapes=scratch,
        cost_estimate=pl.CostEstimate(flops=flops, bytes_accessed=nbytes, transcendentals=trans),
        compiler_params=pltpu.CompilerParams(vmem_limit_bytes=48 * 2**20),
    )


def sds(*shape, dtype=BF):
    return jax.ShapeDtypeStruct(shape, dtype)


def normed(h, scale, shift):
    x = h.astype(F32)
    mean = jnp.mean(x, axis=-1, keepdims=True)
    x = x - mean
    var = jnp.mean(x * x, axis=-1, keepdims=True)
    return (x * lax.rsqrt(var + 1e-06) * (1.0 + scale) + shift).astype(BF)


def gated(h, gate, branch):
    return (h.astype(F32) + gate * branch.astype(F32)).astype(BF)


def first_kernel(lat, cache, mods, h_out, modin_out):
    h = gated(lat[...], mods[2:3], cache[...])
    h_out[...] = h
    modin = normed(h, mods[4:5], mods[3:4]).astype(F32)
    by_dest = jnp.transpose(modin.reshape(2, 16, 8, D), (1, 0, 2, 3))
    modin_out[...] = by_dest.reshape(16, 16, D).astype(BF)


def middle_kernel(h1, chunks, mods, nt_out, h_out, modin_out):
    nt = chunks[...].astype(F32).reshape(16, 2, 8, D)
    nt = jnp.transpose(nt, (1, 0, 2, 3)).reshape(TOK, D).astype(BF)
    nt_out[...] = nt
    h = gated(h1[...], mods[5:6], nt)
    h_out[...] = h
    modin_out[...] = normed(h, mods[7:8], mods[6:7])


def project(flags, x_own, x_other, w_own, w_a, w_b, w_all, y_t):
    w_all[:HALF] = w_own[...]
    w_all[HALF : HALF + 288] = w_a[...]
    w_all[HALF + 288 :] = w_b[...]
    x = jnp.concatenate([x_own[...], x_other[...]], axis=0)
    low, high = x[:, :HALF], x[:, HALF:]
    swap = flags[0] == 1
    x = jnp.concatenate([jnp.where(swap, high, low), jnp.where(swap, low, high)], axis=1)
    for start in range(0, QKV, 256):
        stop = min(start + 256, QKV)
        y = jnp.dot(x, w_all[:, start:stop], preferred_element_type=F32)
        y_t[start:stop] = y.T


def unit(v, factor):
    mean = jnp.mean(v * v, axis=0, keepdims=True)
    return (v * (lax.rsqrt(mean + 1e-06) * factor)).astype(BF)


def head_qkv(y_t, head):
    base = head * 3 * HD
    return (
        unit(y_t[base : base + HD], SCALE),
        unit(y_t[base + HD : base + 2 * HD], 1.0),
        y_t[base + 2 * HD : base + 3 * HD].astype(BF),
    )


def spatial_qkv_kernel(flags, x_own, x_other, w_own, w_a, w_b, out, w_all, y_t):
    project(flags, x_own, x_other, w_own, w_a, w_b, w_all, y_t)
    for head in range(8):
        q, k, v = head_qkv(y_t, head)
        out[head, 0] = q
        out[head, 1] = k
        out[head, 2] = v


def attend(k, q, v, mask=None):
    s = lax.dot_general(k, q, (((0,), (0,)), ((), ())), preferred_element_type=F32)
    p = jnp.exp2(s)
    if mask is not None:
        p = jnp.where(mask, p, 0.0)
    total = jnp.sum(p, axis=0, keepdims=True)
    o = jnp.dot(v, p.astype(BF), preferred_element_type=F32)
    return (o * (1.0 / total)).astype(BF)


def temporal_kernel(flags, x_own, x_other, w_own, w_a, w_b, own_out, other_out, w_all, y_t):
    project(flags, x_own, x_other, w_own, w_a, w_b, w_all, y_t)
    key = lax.broadcasted_iota(jnp.int32, (TOK, TOK), 0)
    query = lax.broadcasted_iota(jnp.int32, (TOK, TOK), 1)
    mask = (key & 15) == (query & 15)
    for head in range(8):
        q, k, v = head_qkv(y_t, head)
        own_out[head] = attend(k[:, :TOK], q[:, :TOK], v[:, :TOK], mask)
        other_out[head] = attend(k[:, TOK:], q[:, TOK:], v[:, TOK:], mask)


def spatial_kernel(q_ref, all_ref, out, keys, values):
    @pl.when(pl.program_id(0) == 0)
    def _():
        for b in range(2):
            for src in range(8):
                for rel in range(2):
                    lanes = slice(rel * 256 + b * 128, rel * 256 + b * 128 + 128)
                    rows = slice(src * 256 + rel * 128, src * 256 + rel * 128 + 128)
                    keys[b, rows] = all_ref[src, 1, :, lanes].astype(F32).T.astype(BF)
                    values[b, :, rows] = all_ref[src, 2, :, lanes]

    for b in range(2):
        parts = [q_ref[0, 0, :, rel * 256 + b * 128 : rel * 256 + b * 128 + 128] for rel in range(2)]
        q = jnp.concatenate(parts, axis=1)
        s = jnp.dot(keys[b], q, preferred_element_type=F32)
        p = jnp.exp2(s)
        total = jnp.sum(p, axis=0, keepdims=True)
        o = jnp.dot(values[b], p.astype(BF), preferred_element_type=F32)
        o = (o * (1.0 / total)).astype(BF)
        for rel in range(2):
            out[0, :, rel * 256 + b * 128 : rel * 256 + b * 128 + 128] = o[:, rel * 128 : rel * 128 + 128]


def spatial_attend(packed):
    return pl.pallas_call(
        spatial_kernel,
        name="spatial_attend",
        grid=(8,),
        out_shape=sds(8, HD, 512),
        in_specs=[
            pl.BlockSpec((1, 3, HD, 512), lambda j: (j, 0, 0, 0)),
            pl.BlockSpec((8, 3, HD, 512), lambda j: (0, 0, 0, 0)),
        ],
        out_specs=pl.BlockSpec((1, HD, 512), lambda j: (j, 0, 0)),
        scratch_shapes=[pltpu.VMEM((2, 2048, HD), BF), pltpu.VMEM((2, HD, 2048), BF)],
        cost_estimate=pl.CostEstimate(flops=2 * 2**34, bytes_accessed=3 * 2**20, transcendentals=2**23),
        compiler_params=pltpu.CompilerParams(vmem_limit_bytes=48 * 2**20),
    )(packed, packed)


def out_project(flags, a_own, a_rec, w_mine, w_partner):
    same = flags[0] == flags[1]
    mine, received = a_own[...], a_rec[...]
    a = jnp.concatenate([jnp.where(same, mine, received), jnp.where(same, received, mine)], axis=0)
    a = a.astype(F32).T.astype(BF)
    halves = []
    for own, other_a, other_b in (w_mine, w_partner):
        w = jnp.concatenate([own[...], other_a[...], other_b[...]], axis=0)
        halves.append(jnp.dot(a, w, preferred_element_type=F32).astype(BF))
    first = flags[1] == 0
    return jnp.concatenate(
        [jnp.where(first, halves[0], halves[1]), jnp.where(first, halves[1], halves[0])], axis=1
    )


def temporal_out_kernel(flags, a_own, a_rec, m0, m1, m2, p0, p1, p2, out):
    out[...] = out_project(flags, a_own, a_rec, (m0, m1, m2), (p0, p1, p2))


def last_kernel(flags, a_own, a_rec, m0, m1, m2, p0, p1, p2, h2, nt, mods, block_out, ns_out):
    ns = out_project(flags, a_own, a_rec, (m0, m1, m2), (p0, p1, p2))
    ns_out[...] = ns
    h = gated(h2[...], mods[8:9], ns)
    block_out[...] = gated(h, mods[11:12], nt[...])


def core_swap(a):
    return lax.ppermute(a, "c", CORE)


def half_columns(w, c):
    low = jnp.concatenate([w[:, :QKV], w[:, 3 * D : 3 * D + HALF]], axis=1)
    high = jnp.concatenate([w[:, QKV : 3 * D], w[:, 3 * D + HALF :]], axis=1)
    return jnp.where(c == 0, low, high)


def from_x(own):
    return (
        own,
        lax.ppermute(own[:288], XX, X_UP),
        lax.ppermute(own[288:], XX, X_DOWN),
    )


def after(value, *deps):
    return lax.optimization_barrier((value, *deps))[0]


def shards(latent, spatial_cache, modulation, weights):
    c, xl = lax.axis_index("c"), lax.axis_index("xl")
    flags = jnp.stack([xl, c]).astype(jnp.int32)
    mods = modulation.reshape(12, D)
    w1 = lax.all_gather(half_columns(weights[1], c), "z", axis=0, tiled=True)
    w0 = lax.all_gather(half_columns(weights[0], c), "z", axis=0, tiled=True)

    h1, modin = call(first_kernel, "first", (sds(TOK, D), sds(16, 16, D)), [VMEM] * 3, nbytes=2**21)(
        latent.reshape(TOK, D), spatial_cache.reshape(TOK, D), mods
    )
    modin = lax.all_to_all(modin, TM, 0, 0, tiled=True).reshape(TOK, D)
    modin_other = core_swap(modin)

    scratch = [pltpu.VMEM((D, QKV), BF), pltpu.VMEM((QKV, 512), F32)]
    w1_qkv = from_x(w1[:, :QKV])
    w1_out = from_x(after(w1[:, QKV:], *w1_qkv[1:]))
    w1_out_partner = tuple(core_swap(w) for w in w1_out)
    a_own, a_other = call(
        temporal_kernel,
        "temporal",
        (sds(8, HD, TOK), sds(8, HD, TOK)),
        [SMEM] + [VMEM] * 5,
        scratch,
        flops=2 * 2**30,
        nbytes=6 * 2**20,
        trans=2**20,
    )(flags, modin, modin_other, *w1_qkv)
    a_rec = core_swap(a_other)
    nt = call(
        temporal_out_kernel,
        "temporal_out",
        sds(TOK, D),
        [SMEM] + [VMEM] * 8,
        flops=2**30,
        nbytes=4 * 2**20,
    )(flags, a_own.reshape(HALF, TOK), a_rec.reshape(HALF, TOK), *w1_out, *w1_out_partner)
    w0 = after(w0, nt)
    w0_qkv = from_x(w0[:, :QKV])
    w0_out = from_x(after(w0[:, QKV:], *w0_qkv[1:]))
    w0_out_partner = tuple(core_swap(w) for w in w0_out)

    chunks = lax.all_to_all(nt.reshape(16, 16, D), TM, 0, 0, tiled=True)
    nt, h2, modin = call(
        middle_kernel, "middle", (sds(TOK, D), sds(TOK, D), sds(TOK, D)), [VMEM] * 3, nbytes=2**21
    )(h1, chunks, mods)
    modin_other = core_swap(modin)
    packed = call(
        spatial_qkv_kernel,
        "spatial_qkv",
        sds(8, 3, HD, 512),
        [SMEM] + [VMEM] * 5,
        scratch,
        flops=2 * 2**30,
        nbytes=6 * 2**20,
    )(flags, modin, modin_other, *w0_qkv)
    packed = lax.all_to_all(packed, ("xh", "y"), 0, 0, tiled=True)
    attn = spatial_attend(packed)
    attn = lax.all_to_all(attn, ("xh", "y"), 0, 0, tiled=True).reshape(HALF, 512)
    a_rec = core_swap(attn[:, TOK:])
    block_out, ns = call(
        last_kernel,
        "last",
        (sds(TOK, D), sds(TOK, D)),
        [SMEM] + [VMEM] * 11,
        flops=2**30,
        nbytes=6 * 2**20,
    )(flags, attn[:, :TOK], a_rec, *w0_out, *w0_out_partner, h2, nt, mods)
    whole = (2, 1, 128, D)
    return block_out.reshape(whole), ns.reshape(whole), nt.reshape(whole)


def solution(mesh):
    fine = Mesh(mesh.devices.reshape(2, 8, 2, 4, 2), ("xl", "z", "xh", "y", "c"))
    tokens = P(None, TM, SPACE, None)
    return jax.shard_map(
        shards,
        mesh=fine,
        in_specs=(tokens, tokens, P(), P(None, TM, None)),
        out_specs=(tokens, tokens, tokens),
        check_vma=False,
    )
```

```python
import math

import jax
import jax.numpy as jnp
from jax import lax
from jax.experimental import pallas as pl
from jax.experimental.pallas import tpu as pltpu
from jax.sharding import Mesh, PartitionSpec as P

D = 1152
HD = 72
HALF = D // 2
QKV = 3 * HALF
WIDE = QKV // 2
PAD = 896
BOTH = 1536
TOK = 256
SCALE = math.log2(math.e) / math.sqrt(HD)
TM = ("xl", "z")
SPACE = ("xh", "y", "c")
XX = ("xl", "xh")
BF = jnp.bfloat16
F32 = jnp.float32
VMEM = pl.BlockSpec(memory_space=pltpu.VMEM)
SMEM = pl.BlockSpec(memory_space=pltpu.SMEM)


def x_pairs(step):
    place = lambda x: (x % 2) * 2 + x // 2
    return [(place(x), place((x + step) % 4)) for x in range(4)]


CORE = [(0, 1), (1, 0)]
Y_UP = [(i, (i + 1) % 4) for i in range(4)]
Y_DOWN = [(i, (i - 1) % 4) for i in range(4)]
X_UP, X_DOWN = x_pairs(1), x_pairs(-1)


def call(body, name, outs, ins, scratch=(), flops=0, nbytes=0, trans=0):
    return pl.pallas_call(
        body,
        name=name,
        out_shape=outs,
        in_specs=ins,
        out_specs=jax.tree.map(lambda _: VMEM, outs),
        scratch_shapes=scratch,
        cost_estimate=pl.CostEstimate(flops=flops, bytes_accessed=nbytes, transcendentals=trans),
        compiler_params=pltpu.CompilerParams(vmem_limit_bytes=24 * 2**20),
    )


def sds(*shape, dtype=BF):
    return jax.ShapeDtypeStruct(shape, dtype)


def normed(h, scale, shift):
    x = h.astype(F32)
    mean = jnp.mean(x, axis=-1, keepdims=True)
    x = x - mean
    var = jnp.mean(x * x, axis=-1, keepdims=True)
    return (x * lax.rsqrt(var + 1e-06) * (1.0 + scale) + shift).astype(BF)


def gated(h, gate, branch):
    return (h.astype(F32) + gate * branch.astype(F32)).astype(BF)


def prepare_kernel(flags, w, first_out, second_out, third_out):
    c, color = flags[1], flags[2]

    def choose(layer, start, width, count, index):
        part = w[layer, :, start : start + width]
        for i in range(1, count):
            part = jnp.where(index == i, w[layer, :, start + i * width : start + (i + 1) * width], part)
        return part

    first_out[...] = choose(1, 0, QKV, 2, c)
    second_out[:, :WIDE] = choose(0, 0, WIDE, 4, 2 * c + color)
    second_out[:, WIDE:PAD] = jnp.zeros((HD, PAD - WIDE), BF)
    second_out[:, PAD : PAD + HALF] = choose(1, 3 * D, HALF, 2, c)
    second_out[:, PAD + HALF :] = jnp.zeros((HD, BOTH - PAD - HALF), BF)
    third_out[...] = w[0, :, 3 * D :]


def first_kernel(lat, cache, mods, h_out, modin_out):
    h = gated(lat[...], mods[2:3], cache[...])
    h_out[...] = h
    modin = normed(h, mods[4:5], mods[3:4]).astype(F32)
    by_dest = jnp.transpose(modin.reshape(2, 16, 8, D), (1, 0, 2, 3))
    modin_out[...] = by_dest.reshape(16, 16, D).astype(BF)


def multiply(x, w_all, y_t):
    width = w_all.shape[1]
    for start in range(0, width, 256):
        stop = min(start + 256, width)
        y = jnp.dot(x, w_all[:, start:stop], preferred_element_type=F32)
        y_t[start:stop] = y.T


def own_first(x, flags):
    low, high = x[:, :HALF], x[:, HALF:]
    swap = flags[0] == 1
    return jnp.concatenate([jnp.where(swap, high, low), jnp.where(swap, low, high)], axis=1)


def unit(v, factor):
    mean = jnp.mean(v * v, axis=0, keepdims=True)
    return (v * (lax.rsqrt(mean + 1e-06) * factor)).astype(BF)


def head_qkv(y_t, head):
    base = head * 3 * HD
    return (
        unit(y_t[base : base + HD], SCALE),
        unit(y_t[base + HD : base + 2 * HD], 1.0),
        y_t[base + 2 * HD : base + 3 * HD].astype(BF),
    )


def project(x_own, x_other, gathered, low, high, w_all, y_t):
    x = jnp.concatenate([x_own[...], x_other[...]], axis=0)
    w_all[0, :HALF] = gathered[:, :WIDE]
    w_all[0, HALF:] = gathered[:, BOTH : BOTH + WIDE]
    w_all[1, :HALF] = low[...]
    w_all[1, HALF:] = high[...]
    for group in range(2):
        multiply(x, w_all.at[group], y_t.at[group])


def spatial_qkv_kernel(flags, x_own, x_other, gathered, low, high, out, w_all, y_t):
    project(x_own, x_other, gathered, low, high, w_all, y_t)
    for head in range(8):
        place = 4 * (flags[2] ^ (head // 4)) + head % 4
        q, k, v = head_qkv(y_t.at[head // 4], head % 4)
        out[place, 0] = q
        out[place, 1] = k
        out[place, 2] = v


def attend(k, q, v, mask=None):
    s = lax.dot_general(k, q, (((0,), (0,)), ((), ())), preferred_element_type=F32)
    p = jnp.exp2(s)
    if mask is not None:
        p = jnp.where(mask, p, 0.0)
    total = jnp.sum(p, axis=0, keepdims=True)
    o = jnp.dot(v, p.astype(BF), preferred_element_type=F32)
    return o * (1.0 / total)


def temporal_kernel(flags, x_own, x_other, w_own, w_a, w_b, own_out, other_out, w_all, y_t, o_t):
    w_all[:HALF] = w_own[...]
    w_all[HALF : HALF + 288] = w_a[...]
    w_all[HALF + 288 :] = w_b[...]
    multiply(own_first(jnp.concatenate([x_own[...], x_other[...]], axis=0), flags), w_all, y_t)
    key = lax.broadcasted_iota(jnp.int32, (TOK, TOK), 0)
    query = lax.broadcasted_iota(jnp.int32, (TOK, TOK), 1)
    mask = (key & 15) == (query & 15)
    for head in range(8):
        q, k, v = head_qkv(y_t, head)
        o_t[head, :, :TOK] = attend(k[:, :TOK], q[:, :TOK], v[:, :TOK], mask)
        o_t[head, :, TOK:] = attend(k[:, TOK:], q[:, TOK:], v[:, TOK:], mask)
    o = o_t[...].reshape(HALF, 512)
    own_out[...] = o[:, :TOK].T.astype(BF)
    other_out[...] = o[:, TOK:].T.astype(BF)


def spatial_kernel(q_ref, all_ref, out, keys, values):
    @pl.when(pl.program_id(0) == 0)
    def _():
        for b in range(2):
            for src in range(8):
                for rel in range(2):
                    lanes = slice(rel * 256 + b * 128, rel * 256 + b * 128 + 128)
                    rows = slice(src * 256 + rel * 128, src * 256 + rel * 128 + 128)
                    keys[b, rows] = all_ref[src, 1, :, lanes].astype(F32).T.astype(BF)
                    values[b, :, rows] = all_ref[src, 2, :, lanes]

    places = [(j, b) for j in range(2) for b in range(2)]

    def lanes(b, rel):
        return slice(rel * 256 + b * 128, rel * 256 + b * 128 + 128)

    def scores(j, b):
        q = jnp.concatenate([q_ref[j, 0, :, lanes(b, rel)] for rel in range(2)], axis=1)
        return jnp.dot(keys[b], q, preferred_element_type=F32)

    s = scores(*places[0])
    for i, (j, b) in enumerate(places):
        following = scores(*places[i + 1]) if i < 3 else None
        p = jnp.exp2(s)
        total = jnp.sum(p, axis=0, keepdims=True)
        o = jnp.dot(values[b], p.astype(BF), preferred_element_type=F32)
        o = (o * (1.0 / total)).astype(BF)
        for rel in range(2):
            out[j, :, lanes(b, rel)] = o[:, rel * 128 : rel * 128 + 128]
        s = following


def spatial_attend(packed):
    return pl.pallas_call(
        spatial_kernel,
        name="spatial_attend",
        grid=(4,),
        out_shape=sds(8, HD, 512),
        in_specs=[
            pl.BlockSpec((2, 3, HD, 512), lambda j: (j, 0, 0, 0)),
            pl.BlockSpec((8, 3, HD, 512), lambda j: (0, 0, 0, 0)),
        ],
        out_specs=pl.BlockSpec((2, HD, 512), lambda j: (j, 0, 0)),
        scratch_shapes=[pltpu.VMEM((2, 2048, HD), BF), pltpu.VMEM((2, HD, 2048), BF)],
        cost_estimate=pl.CostEstimate(flops=2**33, bytes_accessed=3 * 2**20, transcendentals=2**23),
        compiler_params=pltpu.CompilerParams(vmem_limit_bytes=24 * 2**20),
    )(packed, packed)


def middle_kernel(flags, h1, chunks, m0, m1, p0, p1, mods, nt_out, h_out, modin_out):
    a = jnp.transpose(chunks[...].astype(F32).reshape(16, 2, 8, D), (1, 0, 2, 3)).reshape(TOK, D).astype(BF)
    low, high = a[:, :HALF], a[:, HALF:]
    first = flags[1] == 0
    a = jnp.concatenate([jnp.where(first, low, high), jnp.where(first, high, low)], axis=1)
    halves = []
    for xl0, xl1 in ((m0, m1), (p0, p1)):
        w = jnp.concatenate([xl0[...], xl1[...]], axis=0)
        halves.append(jnp.dot(a, w, preferred_element_type=F32).astype(BF))
    low = jnp.where(first, halves[0], halves[1])
    high = jnp.where(first, halves[1], halves[0])
    nt = jnp.concatenate([low, high], axis=1)
    nt_out[...] = nt
    h = gated(h1[...], mods[5:6], nt)
    h_out[...] = h
    modin_out[...] = normed(h, mods[7:8], mods[6:7])


def last_kernel(flags, a_own, a_rec, w_own, w_a, w_b, h2, nt, mods, block_out, ns_out):
    same = flags[0] == flags[1]
    mine, received = a_own[...], a_rec[...]
    a = jnp.concatenate([jnp.where(same, mine, received), jnp.where(same, received, mine)], axis=0)
    a = a.astype(F32).T.astype(BF)
    w = jnp.concatenate([w_own[...], w_a[...], w_b[...]], axis=0)
    ns = jnp.dot(a, w, preferred_element_type=F32).astype(BF)
    ns_out[...] = ns
    h = gated(h2[...], mods[8:9], ns)
    block_out[...] = gated(h, mods[11:12], nt[...])


def core_swap(a):
    return lax.ppermute(a, "c", CORE)


def from_x(own):
    return (
        own,
        lax.ppermute(own[:288], XX, X_UP),
        lax.ppermute(own[288:], XX, X_DOWN),
    )


def gather_z(w):
    return lax.all_gather(w, "z", axis=0, tiled=True)


def after(value, *deps):
    return lax.optimization_barrier((value, *deps))[0]


def shards(latent, spatial_cache, modulation, weights):
    c, xl, z = lax.axis_index("c"), lax.axis_index("xl"), lax.axis_index("z")
    color = lax.axis_index("y") % 2
    flags = jnp.stack([xl, c, color]).astype(jnp.int32)
    mods = modulation.reshape(12, D)
    first_w, second_w, third_w = call(
        prepare_kernel,
        "prepare",
        (sds(HD, QKV), sds(HD, BOTH), sds(HD, D)),
        [SMEM, VMEM],
        nbytes=2**21,
    )(flags, weights)
    w1_own = gather_z(first_w)
    partner = lax.ppermute(second_w, "xl", CORE)
    low, high = jnp.where(xl == 0, second_w, partner), jnp.where(xl == 0, partner, second_w)
    second_w = gather_z(jnp.concatenate([low, high], axis=1))
    w0_out = gather_z(third_w)

    h1, modin = call(first_kernel, "first", (sds(TOK, D), sds(16, 16, D)), [VMEM] * 3, nbytes=2**21)(
        latent.reshape(TOK, D), spatial_cache.reshape(TOK, D), mods
    )
    w1_qkv = from_x(w1_own)
    modin = after(modin, w1_own)
    modin = lax.all_to_all(modin, TM, 0, 0, tiled=True).reshape(TOK, D)
    modin_other = core_swap(modin)
    own, other = call(
        temporal_kernel,
        "temporal",
        (sds(TOK, HALF), sds(TOK, HALF)),
        [SMEM] + [VMEM] * 5,
        [pltpu.VMEM((D, QKV), BF), pltpu.VMEM((QKV, 512), F32), pltpu.VMEM((8, HD, 512), F32)],
        flops=2 * 2**30,
        nbytes=6 * 2**20,
        trans=2**20,
    )(flags, modin, modin_other, *w1_qkv)
    attn = jnp.concatenate([own, core_swap(other)], axis=1)
    second_w = after(second_w, attn)
    chunks = lax.all_to_all(attn.reshape(16, 16, D), TM, 0, 0, tiled=True)
    w1_out = second_w[:, PAD : PAD + HALF], second_w[:, BOTH + PAD : BOTH + PAD + HALF]
    w1_partner = tuple(core_swap(w) for w in w1_out)
    far = (
        lax.ppermute(second_w[:, :WIDE], "y", Y_UP),
        lax.ppermute(second_w[:, BOTH : BOTH + WIDE], "y", Y_DOWN),
    )
    nt, h2, modin = call(
        middle_kernel,
        "middle",
        (sds(TOK, D), sds(TOK, D), sds(TOK, D)),
        [SMEM] + [VMEM] * 7,
        flops=2**30,
        nbytes=5 * 2**20,
    )(flags, h1, chunks, *w1_out, *w1_partner, mods)
    modin = after(modin, *far)
    modin_other = core_swap(modin)
    packed = call(
        spatial_qkv_kernel,
        "spatial_qkv",
        sds(8, 3, HD, 512),
        [SMEM] + [VMEM] * 5,
        [pltpu.VMEM((2, D, WIDE), BF), pltpu.VMEM((2, WIDE, 512), F32)],
        flops=2 * 2**30,
        nbytes=6 * 2**20,
    )(flags, modin, modin_other, second_w, *far)
    packed = lax.all_to_all(packed, ("xh", "y"), 0, 0, tiled=True)
    w0_out = from_x(after(w0_out, packed))
    attn = after(spatial_attend(packed), *w0_out)
    attn = lax.all_to_all(attn, ("xh", "y"), 0, 0, tiled=True).reshape(HALF, 512)
    a_rec = core_swap(attn[:, TOK:])
    block_out, ns = call(
        last_kernel,
        "last",
        (sds(TOK, D), sds(TOK, D)),
        [SMEM] + [VMEM] * 8,
        flops=2**30,
        nbytes=6 * 2**20,
    )(flags, attn[:, :TOK], a_rec, *w0_out, h2, nt, mods)
    whole = (2, 1, 128, D)
    return block_out.reshape(whole), ns.reshape(whole), nt.reshape(whole)


def solution(mesh):
    fine = Mesh(mesh.devices.reshape(2, 8, 2, 4, 2), ("xl", "z", "xh", "y", "c"))
    tokens = P(None, TM, SPACE, None)
    return jax.shard_map(
        shards,
        mesh=fine,
        in_specs=(tokens, tokens, P(), P(None, TM, None)),
        out_specs=(tokens, tokens, tokens),
        check_vma=False,
    )
```

```python
import math

import jax
import jax.numpy as jnp
from jax import lax
from jax.experimental import pallas as pl
from jax.experimental.pallas import tpu as pltpu
from jax.sharding import Mesh, PartitionSpec as P

D = 1152
HD = 72
HALF = D // 2
QKV = 3 * HALF
WIDE = QKV // 2
PAD = 896
BOTH = 1536
LAST = 640
TOK = 256
SCALE = math.log2(math.e) / math.sqrt(HD)
TM = ("xl", "z")
SPACE = ("xh", "y", "c")
XX = ("xl", "xh")
BF = jnp.bfloat16
F32 = jnp.float32
VMEM = pl.BlockSpec(memory_space=pltpu.VMEM)
SMEM = pl.BlockSpec(memory_space=pltpu.SMEM)


def x_pairs(step):
    place = lambda x: (x % 2) * 2 + x // 2
    return [(place(x), place((x + step) % 4)) for x in range(4)]


CORE = [(0, 1), (1, 0)]
Y_UP = [(i, (i + 1) % 4) for i in range(4)]
Y_DOWN = [(i, (i - 1) % 4) for i in range(4)]
X_UP, X_DOWN = x_pairs(1), x_pairs(-1)


def call(body, name, outs, ins, scratch=(), flops=0, nbytes=0, trans=0):
    return pl.pallas_call(
        body,
        name=name,
        out_shape=outs,
        in_specs=ins,
        out_specs=jax.tree.map(lambda _: VMEM, outs),
        scratch_shapes=scratch,
        cost_estimate=pl.CostEstimate(flops=flops, bytes_accessed=nbytes, transcendentals=trans),
        compiler_params=pltpu.CompilerParams(vmem_limit_bytes=24 * 2**20),
    )


def sds(*shape, dtype=BF):
    return jax.ShapeDtypeStruct(shape, dtype)


def normed(h, scale, shift):
    x = h.astype(F32)
    mean = jnp.mean(x, axis=-1, keepdims=True)
    x = x - mean
    var = jnp.mean(x * x, axis=-1, keepdims=True)
    return (x * lax.rsqrt(var + 1e-06) * (1.0 + scale) + shift).astype(BF)


def gated(h, gate, branch):
    return (h.astype(F32) + gate * branch.astype(F32)).astype(BF)


def prepare_kernel(flags, w, first_out, second_out, third_out):
    c, color = flags[1], flags[2]

    def choose(layer, start, width, count, index):
        part = w[layer, :, start : start + width]
        for i in range(1, count):
            part = jnp.where(index == i, w[layer, :, start + i * width : start + (i + 1) * width], part)
        return part

    first_out[...] = choose(1, 0, QKV, 2, c)
    second_out[:, :WIDE] = choose(0, 0, WIDE, 4, 2 * c + color)
    second_out[:, WIDE:PAD] = jnp.zeros((HD, PAD - WIDE), BF)
    second_out[:, PAD : PAD + HALF] = choose(1, 3 * D, HALF, 2, c)
    second_out[:, PAD + HALF :] = jnp.zeros((HD, BOTH - PAD - HALF), BF)
    third_out[:, :HALF] = choose(0, 3 * D, HALF, 2, c)
    third_out[:, HALF:] = jnp.zeros((HD, LAST - HALF), BF)


def first_kernel(lat, cache, mods, h_out, modin_out):
    h = gated(lat[...], mods[2:3], cache[...])
    h_out[...] = h
    modin = normed(h, mods[4:5], mods[3:4]).astype(F32)
    by_dest = jnp.transpose(modin.reshape(2, 16, 8, D), (1, 0, 2, 3))
    modin_out[...] = by_dest.reshape(16, 16, D).astype(BF)


def multiply(x, w_all, y_t):
    width = w_all.shape[1]
    for start in range(0, width, 256):
        stop = min(start + 256, width)
        y = jnp.dot(x, w_all[:, start:stop], preferred_element_type=F32)
        y_t[start:stop] = y.T


def own_first(x, flags):
    low, high = x[:, :HALF], x[:, HALF:]
    swap = flags[0] == 1
    return jnp.concatenate([jnp.where(swap, high, low), jnp.where(swap, low, high)], axis=1)


def unit(v, factor):
    mean = jnp.mean(v * v, axis=0, keepdims=True)
    return (v * (lax.rsqrt(mean + 1e-06) * factor)).astype(BF)


def head_qkv(y_t, head):
    base = head * 3 * HD
    return (
        unit(y_t[base : base + HD], SCALE),
        unit(y_t[base + HD : base + 2 * HD], 1.0),
        y_t[base + 2 * HD : base + 3 * HD].astype(BF),
    )


def project(x_own, x_other, gathered, low, high, w_all, y_t):
    x = jnp.concatenate([x_own[...], x_other[...]], axis=0)
    w_all[0, :HALF] = gathered[:, :WIDE]
    w_all[0, HALF:] = gathered[:, BOTH : BOTH + WIDE]
    w_all[1, :HALF] = low[...]
    w_all[1, HALF:] = high[...]
    for group in range(2):
        multiply(x, w_all.at[group], y_t.at[group])


def spatial_qkv_kernel(flags, x_own, x_other, gathered, low, high, out, w_all, y_t):
    project(x_own, x_other, gathered, low, high, w_all, y_t)
    for head in range(8):
        place = 4 * (flags[2] ^ (head // 4)) + head % 4
        q, k, v = head_qkv(y_t.at[head // 4], head % 4)
        out[place, 0] = q
        out[place, 1] = k
        out[place, 2] = v


def attend(k, q, v, mask=None):
    s = lax.dot_general(k, q, (((0,), (0,)), ((), ())), preferred_element_type=F32)
    p = jnp.exp2(s)
    if mask is not None:
        p = jnp.where(mask, p, 0.0)
    total = jnp.sum(p, axis=0, keepdims=True)
    o = jnp.dot(v, p.astype(BF), preferred_element_type=F32)
    return o * (1.0 / total)


def temporal_kernel(flags, x_own, x_other, w_own, w_a, w_b, own_out, other_out, w_all, y_t, o_t):
    w_all[:HALF] = w_own[...]
    w_all[HALF : HALF + 288] = w_a[...]
    w_all[HALF + 288 :] = w_b[...]
    multiply(own_first(jnp.concatenate([x_own[...], x_other[...]], axis=0), flags), w_all, y_t)
    key = lax.broadcasted_iota(jnp.int32, (TOK, TOK), 0)
    query = lax.broadcasted_iota(jnp.int32, (TOK, TOK), 1)
    mask = (key & 15) == (query & 15)
    for head in range(8):
        q, k, v = head_qkv(y_t, head)
        o_t[head, :, :TOK] = attend(k[:, :TOK], q[:, :TOK], v[:, :TOK], mask)
        o_t[head, :, TOK:] = attend(k[:, TOK:], q[:, TOK:], v[:, TOK:], mask)
    o = o_t[...].reshape(HALF, 512)
    own_out[...] = o[:, :TOK].T.astype(BF)
    other_out[...] = o[:, TOK:].T.astype(BF)


def spatial_kernel(q_ref, all_ref, out, keys, values):
    @pl.when(pl.program_id(0) == 0)
    def _():
        for b in range(2):
            for src in range(8):
                for rel in range(2):
                    lanes = slice(rel * 256 + b * 128, rel * 256 + b * 128 + 128)
                    rows = slice(src * 256 + rel * 128, src * 256 + rel * 128 + 128)
                    keys[b, rows] = all_ref[src, 1, :, lanes].astype(F32).T.astype(BF)
                    values[b, :, rows] = all_ref[src, 2, :, lanes]

    places = [(j, b) for j in range(2) for b in range(2)]

    def lanes(b, rel):
        return slice(rel * 256 + b * 128, rel * 256 + b * 128 + 128)

    def scores(j, b):
        q = jnp.concatenate([q_ref[j, 0, :, lanes(b, rel)] for rel in range(2)], axis=1)
        return jnp.dot(keys[b], q, preferred_element_type=F32)

    s = scores(*places[0])
    for i, (j, b) in enumerate(places):
        following = scores(*places[i + 1]) if i < 3 else None
        p = jnp.exp2(s)
        total = jnp.sum(p, axis=0, keepdims=True)
        o = jnp.dot(values[b], p.astype(BF), preferred_element_type=F32)
        o = (o * (1.0 / total)).astype(BF)
        for rel in range(2):
            out[j, :, lanes(b, rel)] = o[:, rel * 128 : rel * 128 + 128]
        s = following


def spatial_attend(packed):
    return pl.pallas_call(
        spatial_kernel,
        name="spatial_attend",
        grid=(4,),
        out_shape=sds(8, HD, 512),
        in_specs=[
            pl.BlockSpec((2, 3, HD, 512), lambda j: (j, 0, 0, 0)),
            pl.BlockSpec((8, 3, HD, 512), lambda j: (0, 0, 0, 0)),
        ],
        out_specs=pl.BlockSpec((2, HD, 512), lambda j: (j, 0, 0)),
        scratch_shapes=[pltpu.VMEM((2, 2048, HD), BF), pltpu.VMEM((2, HD, 2048), BF)],
        cost_estimate=pl.CostEstimate(flops=2**33, bytes_accessed=3 * 2**20, transcendentals=2**23),
        compiler_params=pltpu.CompilerParams(vmem_limit_bytes=24 * 2**20),
    )(packed, packed)


def out_dot(flags, a, w_mine, w_partner):
    halves = []
    for xl0, xl1 in (w_mine, w_partner):
        w = jnp.concatenate([xl0[...], xl1[...]], axis=0)
        halves.append(jnp.dot(a, w, preferred_element_type=F32).astype(BF))
    first = flags[1] == 0
    low = jnp.where(first, halves[0], halves[1])
    high = jnp.where(first, halves[1], halves[0])
    return jnp.concatenate([low, high], axis=1)


def middle_kernel(flags, h1, chunks, m0, m1, p0, p1, mods, nt_out, h_out, modin_out):
    a = jnp.transpose(chunks[...].astype(F32).reshape(16, 2, 8, D), (1, 0, 2, 3)).reshape(TOK, D).astype(BF)
    low, high = a[:, :HALF], a[:, HALF:]
    first = flags[1] == 0
    a = jnp.concatenate([jnp.where(first, low, high), jnp.where(first, high, low)], axis=1)
    nt = out_dot(flags, a, (m0, m1), (p0, p1))
    nt_out[...] = nt
    h = gated(h1[...], mods[5:6], nt)
    h_out[...] = h
    modin_out[...] = normed(h, mods[7:8], mods[6:7])


def last_kernel(flags, a_own, a_rec, m0, m1, p0, p1, h2, nt, mods, block_out, ns_out):
    first = flags[1] == 0
    mine, received = a_own[...], a_rec[...]
    a = jnp.concatenate([jnp.where(first, mine, received), jnp.where(first, received, mine)], axis=0)
    ns = out_dot(flags, a.astype(F32).T.astype(BF), (m0, m1), (p0, p1))
    ns_out[...] = ns
    h = gated(h2[...], mods[8:9], ns)
    block_out[...] = gated(h, mods[11:12], nt[...])


def core_swap(a):
    return lax.ppermute(a, "c", CORE)


def from_x(own):
    return (
        own,
        lax.ppermute(own[:288], XX, X_UP),
        lax.ppermute(own[288:], XX, X_DOWN),
    )


def both_halves(own, xl):
    other = lax.ppermute(own, "xl", CORE)
    return jnp.concatenate([jnp.where(xl == 0, own, other), jnp.where(xl == 0, other, own)], axis=1)


def gather_z(w):
    return lax.all_gather(w, "z", axis=0, tiled=True)


def after(value, *deps):
    return lax.optimization_barrier((value, *deps))[0]


def shards(latent, spatial_cache, modulation, weights):
    c, xl, z = lax.axis_index("c"), lax.axis_index("xl"), lax.axis_index("z")
    color = lax.axis_index("y") % 2
    flags = jnp.stack([xl, c, color]).astype(jnp.int32)
    mods = modulation.reshape(12, D)
    first_w, second_w, third_w = call(
        prepare_kernel,
        "prepare",
        (sds(HD, QKV), sds(HD, BOTH), sds(HD, LAST)),
        [SMEM, VMEM],
        nbytes=2**21,
    )(flags, weights)
    w1_own = gather_z(first_w)
    second_w = gather_z(both_halves(second_w, xl))
    third_w = gather_z(both_halves(third_w, xl))

    h1, modin = call(first_kernel, "first", (sds(TOK, D), sds(16, 16, D)), [VMEM] * 3, nbytes=2**21)(
        latent.reshape(TOK, D), spatial_cache.reshape(TOK, D), mods
    )
    w1_qkv = from_x(w1_own)
    modin = after(modin, w1_own)
    modin = lax.all_to_all(modin, TM, 0, 0, tiled=True).reshape(TOK, D)
    modin_other = core_swap(modin)
    own, other = call(
        temporal_kernel,
        "temporal",
        (sds(TOK, HALF), sds(TOK, HALF)),
        [SMEM] + [VMEM] * 5,
        [pltpu.VMEM((D, QKV), BF), pltpu.VMEM((QKV, 512), F32), pltpu.VMEM((8, HD, 512), F32)],
        flops=2 * 2**30,
        nbytes=6 * 2**20,
        trans=2**20,
    )(flags, modin, modin_other, *w1_qkv)
    attn = jnp.concatenate([own, core_swap(other)], axis=1)
    second_w = after(second_w, attn)
    chunks = lax.all_to_all(attn.reshape(16, 16, D), TM, 0, 0, tiled=True)
    w1_out = second_w[:, PAD : PAD + HALF], second_w[:, BOTH + PAD : BOTH + PAD + HALF]
    w1_partner = tuple(core_swap(w) for w in w1_out)
    far = (
        lax.ppermute(second_w[:, :WIDE], "y", Y_UP),
        lax.ppermute(second_w[:, BOTH : BOTH + WIDE], "y", Y_DOWN),
    )
    nt, h2, modin = call(
        middle_kernel,
        "middle",
        (sds(TOK, D), sds(TOK, D), sds(TOK, D)),
        [SMEM] + [VMEM] * 7,
        flops=2**30,
        nbytes=5 * 2**20,
    )(flags, h1, chunks, *w1_out, *w1_partner, mods)
    modin = after(modin, far[0])
    modin_other = core_swap(modin)
    packed = call(
        spatial_qkv_kernel,
        "spatial_qkv",
        sds(8, 3, HD, 512),
        [SMEM] + [VMEM] * 5,
        [pltpu.VMEM((2, D, WIDE), BF), pltpu.VMEM((2, WIDE, 512), F32)],
        flops=2 * 2**30,
        nbytes=6 * 2**20,
    )(flags, modin, modin_other, second_w, *far)
    packed = lax.all_to_all(packed, ("xh", "y"), 0, 0, tiled=True)
    attn = spatial_attend(packed)
    w0_out = third_w[:, :HALF], third_w[:, LAST : LAST + HALF]
    w0_partner = tuple(core_swap(w) for w in w0_out)
    attn = lax.all_to_all(attn, ("xh", "y"), 0, 0, tiled=True).reshape(HALF, 512)
    a_rec = core_swap(attn[:, TOK:])
    block_out, ns = call(
        last_kernel,
        "last",
        (sds(TOK, D), sds(TOK, D)),
        [SMEM] + [VMEM] * 9,
        flops=2**30,
        nbytes=6 * 2**20,
    )(flags, attn[:, :TOK], a_rec, *w0_out, *w0_partner, h2, nt, mods)
    whole = (2, 1, 128, D)
    return block_out.reshape(whole), ns.reshape(whole), nt.reshape(whole)


def solution(mesh):
    fine = Mesh(mesh.devices.reshape(2, 8, 2, 4, 2), ("xl", "z", "xh", "y", "c"))
    tokens = P(None, TM, SPACE, None)
    return jax.shard_map(
        shards,
        mesh=fine,
        in_specs=(tokens, tokens, P(), P(None, TM, None)),
        out_specs=(tokens, tokens, tokens),
        check_vma=False,
    )
```

```python
import math

import jax
import jax.numpy as jnp
from jax import lax
from jax.experimental import pallas as pl
from jax.experimental.pallas import tpu as pltpu
from jax.sharding import Mesh, PartitionSpec as P

D = 1152
HD = 72
HALF = D // 2
QKV = 3 * HALF
WIDE = QKV // 2
PAD = 896
BOTH = 1536
LAST = 640
TOK = 256
SCALE = math.log2(math.e) / math.sqrt(HD)
TM = ("xl", "z")
SPACE = ("xh", "y", "c")
XX = ("xl", "xh")
BF = jnp.bfloat16
F32 = jnp.float32
VMEM = pl.BlockSpec(memory_space=pltpu.VMEM)
SMEM = pl.BlockSpec(memory_space=pltpu.SMEM)


def x_pairs(step):
    place = lambda x: (x % 2) * 2 + x // 2
    return [(place(x), place((x + step) % 4)) for x in range(4)]


CORE = [(0, 1), (1, 0)]
Y_UP = [(i, (i + 1) % 4) for i in range(4)]
Y_DOWN = [(i, (i - 1) % 4) for i in range(4)]
X_UP, X_DOWN = x_pairs(1), x_pairs(-1)


def call(body, name, outs, ins, scratch=(), flops=0, nbytes=0, trans=0):
    return pl.pallas_call(
        body,
        name=name,
        out_shape=outs,
        in_specs=ins,
        out_specs=jax.tree.map(lambda _: VMEM, outs),
        scratch_shapes=scratch,
        cost_estimate=pl.CostEstimate(flops=flops, bytes_accessed=nbytes, transcendentals=trans),
        compiler_params=pltpu.CompilerParams(vmem_limit_bytes=24 * 2**20),
    )


def sds(*shape, dtype=BF):
    return jax.ShapeDtypeStruct(shape, dtype)


def normed(h, scale, shift):
    x = h.astype(F32)
    mean = jnp.mean(x, axis=-1, keepdims=True)
    x = x - mean
    var = jnp.mean(x * x, axis=-1, keepdims=True)
    return (x * lax.rsqrt(var + 1e-06) * (1.0 + scale) + shift).astype(BF)


def gated(h, gate, branch):
    return (h.astype(F32) + gate * branch.astype(F32)).astype(BF)


def prepare_kernel(flags, w, first_out, own_out, theirs_out):
    c, color = flags[1], flags[2]

    def choose(layer, start, width, count, index):
        part = w[layer, :, start : start + width]
        for i in range(1, count):
            part = jnp.where(index == i, w[layer, :, start + i * width : start + (i + 1) * width], part)
        return part

    first_out[...] = choose(1, 0, QKV, 2, c)
    w1_half, w0_half = choose(1, 3 * D, HALF, 2, c), choose(0, 3 * D, HALF, 2, c)
    for out, half in ((own_out, color), (theirs_out, 1 - color)):
        out[:, :WIDE] = choose(0, 0, WIDE, 4, 2 * c + half)
        out[:, WIDE:PAD] = jnp.zeros((HD, PAD - WIDE), BF)
        out[:, PAD : PAD + HALF] = w1_half
        out[:, PAD + HALF : BOTH] = jnp.zeros((HD, BOTH - PAD - HALF), BF)
        out[:, BOTH : BOTH + HALF] = w0_half
        out[:, BOTH + HALF :] = jnp.zeros((HD, LAST - HALF), BF)


def join_kernel(flags, own, other, second_out, third_out):
    first = flags[0] == 0
    low, high = jnp.where(first, own[...], other[...]), jnp.where(first, other[...], own[...])
    second_out[:, :BOTH] = low[:, :BOTH]
    second_out[:, BOTH:] = high[:, :BOTH]
    third_out[:, :LAST] = low[:, BOTH:]
    third_out[:, LAST:] = high[:, BOTH:]


def first_kernel(lat, cache, mods, h_out, modin_out):
    h = gated(lat[...], mods[2:3], cache[...])
    h_out[...] = h
    modin = normed(h, mods[4:5], mods[3:4]).astype(F32)
    by_dest = jnp.transpose(modin.reshape(2, 16, 8, D), (1, 0, 2, 3))
    modin_out[...] = by_dest.reshape(16, 16, D).astype(BF)


def multiply(x, w_all, y_t):
    width = w_all.shape[1]
    for start in range(0, width, 256):
        stop = min(start + 256, width)
        y = jnp.dot(x, w_all[:, start:stop], preferred_element_type=F32)
        y_t[start:stop] = y.T


def own_first(x, flags):
    low, high = x[:, :HALF], x[:, HALF:]
    swap = flags[0] == 1
    return jnp.concatenate([jnp.where(swap, high, low), jnp.where(swap, low, high)], axis=1)


def unit(v, factor):
    mean = jnp.mean(v * v, axis=0, keepdims=True)
    return (v * (lax.rsqrt(mean + 1e-06) * factor)).astype(BF)


def head_qkv(y_t, head):
    base = head * 3 * HD
    return (
        unit(y_t[base : base + HD], SCALE),
        unit(y_t[base + HD : base + 2 * HD], 1.0),
        y_t[base + 2 * HD : base + 3 * HD].astype(BF),
    )


def project(x_own, x_other, gathered, blocks, w_all, y_t):
    x = jnp.concatenate([x_own[...], x_other[...]], axis=0)
    w_all[0, :HALF] = gathered[:, :WIDE]
    w_all[0, HALF:] = gathered[:, BOTH : BOTH + WIDE]
    for i, block in enumerate(blocks):
        w_all[1, 288 * i : 288 * i + 288] = block[...]
    for group in range(2):
        multiply(x, w_all.at[group], y_t.at[group])


def spatial_qkv_kernel(flags, x_own, x_other, gathered, f0, f1, f2, f3, out, w_all, y_t):
    project(x_own, x_other, gathered, (f0, f1, f2, f3), w_all, y_t)
    for head in range(8):
        place = 4 * (flags[2] ^ (head // 4)) + head % 4
        q, k, v = head_qkv(y_t.at[head // 4], head % 4)
        out[place, 0] = q
        out[place, 1] = k
        out[place, 2] = v


def temporal_kernel(flags, x_own, x_other, w_own, w_a, w_b, own_out, other_out, w_all, y_t, o_t):
    w_all[:HALF] = w_own[...]
    w_all[HALF : HALF + 288] = w_a[...]
    w_all[HALF + 288 :] = w_b[...]
    multiply(own_first(jnp.concatenate([x_own[...], x_other[...]], axis=0), flags), w_all, y_t)
    key = lax.broadcasted_iota(jnp.int32, (TOK, TOK), 0)
    query = lax.broadcasted_iota(jnp.int32, (TOK, TOK), 1)
    mask = (key & 15) == (query & 15)
    units = [(head, half) for head in range(8) for half in range(2)]
    qkv = {}

    def scores(head, half):
        if half == 0:
            qkv[head] = head_qkv(y_t, head)
        q, k, _ = qkv[head]
        t = slice(half * TOK, half * TOK + TOK)
        return lax.dot_general(k[:, t], q[:, t], (((0,), (0,)), ((), ())), preferred_element_type=F32)

    s = scores(0, 0)
    for i, (head, half) in enumerate(units):
        following = scores(*units[i + 1]) if i < 15 else None
        t = slice(half * TOK, half * TOK + TOK)
        p = jnp.where(mask, jnp.exp2(s), 0.0)
        total = jnp.sum(p, axis=0, keepdims=True)
        o = jnp.dot(qkv[head][2][:, t], p.astype(BF), preferred_element_type=F32)
        o_t[head, :, t] = o * (1.0 / total)
        s = following
    o = o_t[...].reshape(HALF, 512)
    own_out[...] = o[:, :TOK].T.astype(BF)
    other_out[...] = o[:, TOK:].T.astype(BF)


def spatial_kernel(q_ref, all_ref, out, keys, values):
    @pl.when(pl.program_id(0) == 0)
    def _():
        for b in range(2):
            for src in range(8):
                for rel in range(2):
                    lanes = slice(rel * 256 + b * 128, rel * 256 + b * 128 + 128)
                    rows = slice(src * 256 + rel * 128, src * 256 + rel * 128 + 128)
                    keys[b, rows] = all_ref[src, 1, :, lanes].astype(F32).T.astype(BF)
                    values[b, :, rows] = all_ref[src, 2, :, lanes]

    places = [(j, b) for j in range(2) for b in range(2)]

    def lanes(b, rel):
        return slice(rel * 256 + b * 128, rel * 256 + b * 128 + 128)

    def scores(j, b):
        q = jnp.concatenate([q_ref[j, 0, :, lanes(b, rel)] for rel in range(2)], axis=1)
        return jnp.dot(keys[b], q, preferred_element_type=F32)

    s = scores(*places[0])
    for i, (j, b) in enumerate(places):
        following = scores(*places[i + 1]) if i < 3 else None
        p = jnp.exp2(s)
        total = jnp.sum(p, axis=0, keepdims=True)
        o = jnp.dot(values[b], p.astype(BF), preferred_element_type=F32)
        o = (o * (1.0 / total)).astype(BF)
        for rel in range(2):
            out[j, :, lanes(b, rel)] = o[:, rel * 128 : rel * 128 + 128]
        s = following


def spatial_attend(packed):
    return pl.pallas_call(
        spatial_kernel,
        name="spatial_attend",
        grid=(4,),
        out_shape=sds(8, HD, 512),
        in_specs=[
            pl.BlockSpec((2, 3, HD, 512), lambda j: (j, 0, 0, 0)),
            pl.BlockSpec((8, 3, HD, 512), lambda j: (0, 0, 0, 0)),
        ],
        out_specs=pl.BlockSpec((2, HD, 512), lambda j: (j, 0, 0)),
        scratch_shapes=[pltpu.VMEM((2, 2048, HD), BF), pltpu.VMEM((2, HD, 2048), BF)],
        cost_estimate=pl.CostEstimate(flops=2**33, bytes_accessed=3 * 2**20, transcendentals=2**23),
        compiler_params=pltpu.CompilerParams(vmem_limit_bytes=24 * 2**20),
    )(packed, packed)


def out_dot(flags, a_low, a_high, w_mine, w_partner):
    halves = []
    for xl0, xl1 in (w_mine, w_partner):
        low = jnp.dot(a_low, xl0[...], preferred_element_type=F32)
        high = jnp.dot(a_high, xl1[...], preferred_element_type=F32)
        halves.append((low + high).astype(BF))
    first = flags[1] == 0
    low = jnp.where(first, halves[0], halves[1])
    high = jnp.where(first, halves[1], halves[0])
    return jnp.concatenate([low, high], axis=1)


def middle_kernel(flags, h1, chunks, m0, m1, p0, p1, mods, nt_out, h_out, modin_out):
    a = jnp.transpose(chunks[...].astype(F32).reshape(16, 2, 8, D), (1, 0, 2, 3)).reshape(TOK, D).astype(BF)
    low, high = a[:, :HALF], a[:, HALF:]
    first = flags[1] == 0
    nt = out_dot(flags, jnp.where(first, low, high), jnp.where(first, high, low), (m0, m1), (p0, p1))
    nt_out[...] = nt
    h = gated(h1[...], mods[5:6], nt)
    h_out[...] = h
    modin_out[...] = normed(h, mods[7:8], mods[6:7])


def last_kernel(flags, attn, a_rec, m0, m1, p0, p1, h2, nt, mods, block_out, ns_out):
    first = flags[1] == 0
    mine, received = attn[:, :TOK], a_rec[...]
    low = jnp.where(first, mine, received).astype(F32).T.astype(BF)
    high = jnp.where(first, received, mine).astype(F32).T.astype(BF)
    ns = out_dot(flags, low, high, (m0, m1), (p0, p1))
    ns_out[...] = ns
    h = gated(h2[...], mods[8:9], ns)
    block_out[...] = gated(h, mods[11:12], nt[...])


def core_swap(a):
    return lax.ppermute(a, "c", CORE)


def from_x(own):
    return (
        own,
        lax.ppermute(own[:288], XX, X_UP),
        lax.ppermute(own[288:], XX, X_DOWN),
    )


def gather_z(w):
    return lax.all_gather(w, "z", axis=0, tiled=True)


def after(value, *deps):
    return lax.optimization_barrier((value, *deps))[0]


def shards(latent, spatial_cache, modulation, weights):
    c, xl, z = lax.axis_index("c"), lax.axis_index("xl"), lax.axis_index("z")
    color = (lax.axis_index("y") + xl) % 2
    flags = jnp.stack([xl, c, color]).astype(jnp.int32)
    mods = modulation.reshape(12, D)
    first_w, own_w, theirs = call(
        prepare_kernel,
        "prepare",
        (sds(HD, QKV), sds(HD, BOTH + LAST), sds(HD, BOTH + LAST)),
        [SMEM, VMEM],
        nbytes=2**21,
    )(flags, weights)
    w1_own = gather_z(first_w)
    second_w, third_w = call(
        join_kernel, "join", (sds(HD, 2 * BOTH), sds(HD, 2 * LAST)), [SMEM, VMEM, VMEM], nbytes=2**20
    )(flags, own_w, lax.ppermute(theirs, "xl", CORE))
    second_w = gather_z(second_w)

    h1, modin = call(first_kernel, "first", (sds(TOK, D), sds(16, 16, D)), [VMEM] * 3, nbytes=2**21)(
        latent.reshape(TOK, D), spatial_cache.reshape(TOK, D), mods
    )
    w1_qkv = from_x(w1_own)
    modin = after(modin, w1_own)
    modin = lax.all_to_all(modin, TM, 0, 0, tiled=True).reshape(TOK, D)
    modin_other = core_swap(modin)
    own, other = call(
        temporal_kernel,
        "temporal",
        (sds(TOK, HALF), sds(TOK, HALF)),
        [SMEM] + [VMEM] * 5,
        [pltpu.VMEM((D, QKV), BF), pltpu.VMEM((QKV, 512), F32), pltpu.VMEM((8, HD, 512), F32)],
        flops=2 * 2**30,
        nbytes=6 * 2**20,
        trans=2**20,
    )(flags, modin, modin_other, *w1_qkv)
    attn = jnp.concatenate([own, core_swap(other)], axis=1)
    second_w = after(second_w, attn)
    chunks = lax.all_to_all(attn.reshape(16, 16, D), TM, 0, 0, tiled=True)
    low, high = second_w[:, :WIDE], second_w[:, BOTH : BOTH + WIDE]
    far = (
        lax.ppermute(low[:288], "y", Y_UP),
        lax.ppermute(low[288:], "y", Y_DOWN),
        lax.ppermute(high[:288], XX, X_UP),
        lax.ppermute(high[288:], XX, X_DOWN),
    )
    w1_out = second_w[:, PAD : PAD + HALF], second_w[:, BOTH + PAD : BOTH + PAD + HALF]
    w1_partner = tuple(core_swap(w) for w in w1_out)
    nt, h2, modin = call(
        middle_kernel,
        "middle",
        (sds(TOK, D), sds(TOK, D), sds(TOK, D)),
        [SMEM] + [VMEM] * 7,
        flops=2**30,
        nbytes=5 * 2**20,
    )(flags, h1, chunks, *w1_out, *w1_partner, mods)
    modin = after(modin, *far)
    modin_other = core_swap(modin)
    packed = call(
        spatial_qkv_kernel,
        "spatial_qkv",
        sds(8, 3, HD, 512),
        [SMEM] + [VMEM] * 7,
        [pltpu.VMEM((2, D, WIDE), BF), pltpu.VMEM((2, WIDE, 512), F32)],
        flops=2 * 2**30,
        nbytes=6 * 2**20,
    )(flags, modin, modin_other, second_w, *far)
    third_w = gather_z(after(third_w, packed))
    packed = lax.all_to_all(packed, ("xh", "y"), 0, 0, tiled=True)
    attn = spatial_attend(packed)
    w0_out = third_w[:, :HALF], third_w[:, LAST : LAST + HALF]
    w0_partner = tuple(core_swap(w) for w in w0_out)
    attn = lax.all_to_all(attn, ("xh", "y"), 0, 0, tiled=True).reshape(HALF, 512)
    a_rec = core_swap(attn[:, TOK:])
    block_out, ns = call(
        last_kernel,
        "last",
        (sds(TOK, D), sds(TOK, D)),
        [SMEM] + [VMEM] * 9,
        flops=2**30,
        nbytes=6 * 2**20,
    )(flags, attn, a_rec, *w0_out, *w0_partner, h2, nt, mods)
    whole = (2, 1, 128, D)
    return block_out.reshape(whole), ns.reshape(whole), nt.reshape(whole)


def solution(mesh):
    fine = Mesh(mesh.devices.reshape(2, 8, 2, 4, 2), ("xl", "z", "xh", "y", "c"))
    tokens = P(None, TM, SPACE, None)
    return jax.shard_map(
        shards,
        mesh=fine,
        in_specs=(tokens, tokens, P(), P(None, TM, None)),
        out_specs=(tokens, tokens, tokens),
        check_vma=False,
    )
```

```python
import math

import jax
import jax.numpy as jnp
from jax import lax
from jax.experimental import pallas as pl
from jax.experimental.pallas import tpu as pltpu
from jax.sharding import Mesh, PartitionSpec as P

D = 1152
HD = 72
HALF = D // 2
QKV = 3 * HALF
WIDE = QKV // 2
PAD = 896
BOTH = 1536
LAST = 640
TOK = 256
SCALE = math.log2(math.e) / math.sqrt(HD)
TM = ("xl", "z")
SPACE = ("xh", "y", "c")
XX = ("xl", "xh")
BF = jnp.bfloat16
F32 = jnp.float32
VMEM = pl.BlockSpec(memory_space=pltpu.VMEM)
SMEM = pl.BlockSpec(memory_space=pltpu.SMEM)


def x_pairs(step):
    place = lambda x: (x % 2) * 2 + x // 2
    return [(place(x), place((x + step) % 4)) for x in range(4)]


CORE = [(0, 1), (1, 0)]
Y_UP = [(i, (i + 1) % 4) for i in range(4)]
Y_DOWN = [(i, (i - 1) % 4) for i in range(4)]
X_UP, X_DOWN = x_pairs(1), x_pairs(-1)


def call(body, name, outs, ins, scratch=(), flops=0, nbytes=0, trans=0):
    return pl.pallas_call(
        body,
        name=name,
        out_shape=outs,
        in_specs=ins,
        out_specs=jax.tree.map(lambda _: VMEM, outs),
        scratch_shapes=scratch,
        cost_estimate=pl.CostEstimate(flops=flops, bytes_accessed=nbytes, transcendentals=trans),
        compiler_params=pltpu.CompilerParams(vmem_limit_bytes=24 * 2**20),
    )


def sds(*shape, dtype=BF):
    return jax.ShapeDtypeStruct(shape, dtype)


def normed(h, scale, shift):
    x = h.astype(F32)
    mean = jnp.mean(x, axis=-1, keepdims=True)
    x = x - mean
    var = jnp.mean(x * x, axis=-1, keepdims=True)
    return (x * lax.rsqrt(var + 1e-06) * (1.0 + scale) + shift).astype(BF)


def gated(h, gate, branch):
    return (h.astype(F32) + gate * branch.astype(F32)).astype(BF)


def prepare_kernel(flags, w, first_out, own_out, theirs_out):
    c, color = flags[1], flags[2]

    def choose(layer, start, width, count, index):
        part = w[layer, :, start : start + width]
        for i in range(1, count):
            part = jnp.where(index == i, w[layer, :, start + i * width : start + (i + 1) * width], part)
        return part

    first_out[...] = choose(1, 0, QKV, 2, c)
    w1_half, w0_half = choose(1, 3 * D, HALF, 2, c), choose(0, 3 * D, HALF, 2, c)
    for out, half in ((own_out, color), (theirs_out, 1 - color)):
        out[:, :WIDE] = choose(0, 0, WIDE, 4, 2 * c + half)
        out[:, WIDE:PAD] = jnp.zeros((HD, PAD - WIDE), BF)
        out[:, PAD : PAD + HALF] = w1_half
        out[:, PAD + HALF : BOTH] = jnp.zeros((HD, BOTH - PAD - HALF), BF)
        out[:, BOTH : BOTH + HALF] = w0_half
        out[:, BOTH + HALF :] = jnp.zeros((HD, LAST - HALF), BF)


def join_kernel(flags, own, other, second_out, third_out):
    first = flags[0] == 0
    low, high = jnp.where(first, own[...], other[...]), jnp.where(first, other[...], own[...])
    second_out[:, :BOTH] = low[:, :BOTH]
    second_out[:, BOTH:] = high[:, :BOTH]
    third_out[:, :LAST] = low[:, BOTH:]
    third_out[:, LAST:] = high[:, BOTH:]


def first_kernel(lat, cache, mods, h_out, modin_out):
    h = gated(lat[...], mods[2:3], cache[...])
    h_out[...] = h
    modin = normed(h, mods[4:5], mods[3:4]).astype(F32)
    by_dest = jnp.transpose(modin.reshape(2, 16, 8, D), (1, 0, 2, 3))
    modin_out[...] = by_dest.reshape(16, 16, D).astype(BF)


def multiply(x, w_all, y_t):
    width = w_all.shape[1]
    for start in range(0, width, 256):
        stop = min(start + 256, width)
        y = jnp.dot(x, w_all[:, start:stop], preferred_element_type=F32)
        y_t[start:stop] = y.T


def own_first(x, flags):
    low, high = x[:, :HALF], x[:, HALF:]
    swap = flags[0] == 1
    return jnp.concatenate([jnp.where(swap, high, low), jnp.where(swap, low, high)], axis=1)


def unit(v, factor):
    mean = jnp.mean(v * v, axis=0, keepdims=True)
    return (v * (lax.rsqrt(mean + 1e-06) * factor)).astype(BF)


def head_qkv(y_t, head):
    base = head * 3 * HD
    return (
        unit(y_t[base : base + HD], SCALE),
        unit(y_t[base + HD : base + 2 * HD], 1.0),
        y_t[base + 2 * HD : base + 3 * HD].astype(BF),
    )


def project(x_own, x_other, gathered, blocks, w_all, y_t):
    x = jnp.concatenate([x_own[...], x_other[...]], axis=0)
    w_all[0, :HALF] = gathered[:, :WIDE]
    w_all[0, HALF:] = gathered[:, BOTH : BOTH + WIDE]
    for i, block in enumerate(blocks):
        w_all[1, 288 * i : 288 * i + 288] = block[...]
    for group in range(2):
        multiply(x, w_all.at[group], y_t.at[group])


def spatial_qkv_kernel(flags, x_own, x_other, gathered, f0, f1, f2, f3, out, w_all, y_t):
    project(x_own, x_other, gathered, (f0, f1, f2, f3), w_all, y_t)
    for head in range(8):
        place = 4 * (flags[2] ^ (head // 4)) + head % 4
        q, k, v = head_qkv(y_t.at[head // 4], head % 4)
        out[place, 0] = q
        out[place, 1] = k
        out[place, 2] = v


def temporal_kernel(flags, x_own, x_other, w_own, w_a, w_b, own_out, other_out, w_all, y_t, o_t):
    w_all[:HALF] = w_own[...]
    w_all[HALF : HALF + 288] = w_a[...]
    w_all[HALF + 288 :] = w_b[...]
    multiply(own_first(jnp.concatenate([x_own[...], x_other[...]], axis=0), flags), w_all, y_t)
    key = lax.broadcasted_iota(jnp.int32, (TOK, TOK), 0)
    query = lax.broadcasted_iota(jnp.int32, (TOK, TOK), 1)
    mask = (key & 15) == (query & 15)
    units = [(head, half) for head in range(8) for half in range(2)]
    qkv = {}

    def scores(head, half):
        if half == 0:
            qkv[head] = head_qkv(y_t, head)
        q, k, _ = qkv[head]
        t = slice(half * TOK, half * TOK + TOK)
        return lax.dot_general(k[:, t], q[:, t], (((0,), (0,)), ((), ())), preferred_element_type=F32)

    s = scores(0, 0)
    for i, (head, half) in enumerate(units):
        following = scores(*units[i + 1]) if i < 15 else None
        t = slice(half * TOK, half * TOK + TOK)
        p = jnp.where(mask, jnp.exp2(s), 0.0)
        total = jnp.sum(p, axis=0, keepdims=True)
        o = jnp.dot(qkv[head][2][:, t], p.astype(BF), preferred_element_type=F32)
        o_t[head, :, t] = o * (1.0 / total)
        s = following
    o = o_t[...].reshape(HALF, 512)
    own_out[...] = o[:, :TOK].T.astype(BF)
    other_out[...] = o[:, TOK:].T.astype(BF)


def spatial_kernel(q_ref, all_ref, out, keys, values):
    @pl.when(pl.program_id(0) == 0)
    def _():
        for b in range(2):
            for src in range(8):
                for rel in range(2):
                    lanes = slice(rel * 256 + b * 128, rel * 256 + b * 128 + 128)
                    rows = slice(src * 256 + rel * 128, src * 256 + rel * 128 + 128)
                    keys[b, rows] = all_ref[src, 1, :, lanes].astype(F32).T.astype(BF)
                    values[b, :, rows] = all_ref[src, 2, :, lanes]

    places = [(j, b) for j in range(4) for b in range(2)]

    def lanes(b, rel):
        return slice(rel * 256 + b * 128, rel * 256 + b * 128 + 128)

    def scores(j, b):
        q = jnp.concatenate([q_ref[j, 0, :, lanes(b, rel)] for rel in range(2)], axis=1)
        return jnp.dot(keys[b], q, preferred_element_type=F32)

    s = scores(*places[0])
    for i, (j, b) in enumerate(places):
        following = scores(*places[i + 1]) if i < 7 else None
        p = jnp.exp2(s)
        total = jnp.sum(p, axis=0, keepdims=True)
        o = jnp.dot(values[b], p.astype(BF), preferred_element_type=F32)
        o = (o * (1.0 / total)).astype(BF)
        for rel in range(2):
            out[j, :, lanes(b, rel)] = o[:, rel * 128 : rel * 128 + 128]
        s = following


def spatial_attend(packed):
    return pl.pallas_call(
        spatial_kernel,
        name="spatial_attend",
        grid=(2,),
        out_shape=sds(8, HD, 512),
        in_specs=[
            pl.BlockSpec((4, 3, HD, 512), lambda j: (j, 0, 0, 0)),
            pl.BlockSpec((8, 3, HD, 512), lambda j: (0, 0, 0, 0)),
        ],
        out_specs=pl.BlockSpec((4, HD, 512), lambda j: (j, 0, 0)),
        scratch_shapes=[pltpu.VMEM((2, 2048, HD), BF), pltpu.VMEM((2, HD, 2048), BF)],
        cost_estimate=pl.CostEstimate(flops=2**33, bytes_accessed=3 * 2**20, transcendentals=2**23),
        compiler_params=pltpu.CompilerParams(vmem_limit_bytes=24 * 2**20),
    )(packed, packed)


def out_dot(flags, a_low, a_high, w_mine, w_partner):
    halves = []
    for xl0, xl1 in (w_mine, w_partner):
        low = jnp.dot(a_low, xl0[...], preferred_element_type=F32)
        high = jnp.dot(a_high, xl1[...], preferred_element_type=F32)
        halves.append((low + high).astype(BF))
    first = flags[1] == 0
    low = jnp.where(first, halves[0], halves[1])
    high = jnp.where(first, halves[1], halves[0])
    return jnp.concatenate([low, high], axis=1)


def middle_kernel(flags, h1, chunks, m0, m1, p0, p1, mods, nt_out, h_out, modin_out):
    a = jnp.transpose(chunks[...].astype(F32).reshape(16, 2, 8, D), (1, 0, 2, 3)).reshape(TOK, D).astype(BF)
    low, high = a[:, :HALF], a[:, HALF:]
    first = flags[1] == 0
    nt = out_dot(flags, jnp.where(first, low, high), jnp.where(first, high, low), (m0, m1), (p0, p1))
    nt_out[...] = nt
    h = gated(h1[...], mods[5:6], nt)
    h_out[...] = h
    modin_out[...] = normed(h, mods[7:8], mods[6:7])


def last_kernel(flags, attn, a_rec, m0, m1, p0, p1, h2, nt, mods, block_out, ns_out):
    first = flags[1] == 0
    mine, received = attn[:, :TOK], a_rec[...]
    a = jnp.concatenate([jnp.where(first, mine, received), jnp.where(first, received, mine)], axis=0)
    a = a.astype(F32).T.astype(BF)
    halves = []
    for xl0, xl1 in ((m0, m1), (p0, p1)):
        w = jnp.concatenate([xl0[...], xl1[...]], axis=0)
        halves.append(jnp.dot(a, w, preferred_element_type=F32).astype(BF))
    low = jnp.where(first, halves[0], halves[1])
    high = jnp.where(first, halves[1], halves[0])
    ns = jnp.concatenate([low, high], axis=1)
    ns_out[...] = ns
    h = gated(h2[...], mods[8:9], ns)
    block_out[...] = gated(h, mods[11:12], nt[...])


def core_swap(a):
    return lax.ppermute(a, "c", CORE)


def from_x(own):
    return (
        own,
        lax.ppermute(own[:288], XX, X_UP),
        lax.ppermute(own[288:], XX, X_DOWN),
    )


def gather_z(w):
    return lax.all_gather(w, "z", axis=0, tiled=True)


def after(value, *deps):
    return lax.optimization_barrier((value, *deps))[0]


def shards(latent, spatial_cache, modulation, weights):
    c, xl, z = lax.axis_index("c"), lax.axis_index("xl"), lax.axis_index("z")
    color = (lax.axis_index("y") + xl) % 2
    flags = jnp.stack([xl, c, color]).astype(jnp.int32)
    mods = modulation.reshape(12, D)
    first_w, own_w, theirs = call(
        prepare_kernel,
        "prepare",
        (sds(HD, QKV), sds(HD, BOTH + LAST), sds(HD, BOTH + LAST)),
        [SMEM, VMEM],
        nbytes=2**21,
    )(flags, weights)
    w1_own = gather_z(first_w)
    second_w, third_w = call(
        join_kernel, "join", (sds(HD, 2 * BOTH), sds(HD, 2 * LAST)), [SMEM, VMEM, VMEM], nbytes=2**20
    )(flags, own_w, lax.ppermute(theirs, "xl", CORE))
    second_w = gather_z(second_w)

    h1, modin = call(first_kernel, "first", (sds(TOK, D), sds(16, 16, D)), [VMEM] * 3, nbytes=2**21)(
        latent.reshape(TOK, D), spatial_cache.reshape(TOK, D), mods
    )
    w1_qkv = from_x(w1_own)
    modin = after(modin, w1_own)
    modin = lax.all_to_all(modin, TM, 0, 0, tiled=True).reshape(TOK, D)
    modin_other = core_swap(modin)
    own, other = call(
        temporal_kernel,
        "temporal",
        (sds(TOK, HALF), sds(TOK, HALF)),
        [SMEM] + [VMEM] * 5,
        [pltpu.VMEM((D, QKV), BF), pltpu.VMEM((QKV, 512), F32), pltpu.VMEM((8, HD, 512), F32)],
        flops=2 * 2**30,
        nbytes=6 * 2**20,
        trans=2**20,
    )(flags, modin, modin_other, *w1_qkv)
    attn = jnp.concatenate([own, core_swap(other)], axis=1)
    second_w = after(second_w, attn)
    chunks = lax.all_to_all(attn.reshape(16, 16, D), TM, 0, 0, tiled=True)
    low, high = second_w[:, :WIDE], second_w[:, BOTH : BOTH + WIDE]
    far = (
        lax.ppermute(low[:288], "y", Y_UP),
        lax.ppermute(low[288:], "y", Y_DOWN),
        lax.ppermute(high[:288], XX, X_UP),
        lax.ppermute(high[288:], XX, X_DOWN),
    )
    w1_out = second_w[:, PAD : PAD + HALF], second_w[:, BOTH + PAD : BOTH + PAD + HALF]
    w1_partner = tuple(core_swap(w) for w in w1_out)
    nt, h2, modin = call(
        middle_kernel,
        "middle",
        (sds(TOK, D), sds(TOK, D), sds(TOK, D)),
        [SMEM] + [VMEM] * 7,
        flops=2**30,
        nbytes=5 * 2**20,
    )(flags, h1, chunks, *w1_out, *w1_partner, mods)
    modin = after(modin, *far)
    modin_other = core_swap(modin)
    packed = call(
        spatial_qkv_kernel,
        "spatial_qkv",
        sds(8, 3, HD, 512),
        [SMEM] + [VMEM] * 7,
        [pltpu.VMEM((2, D, WIDE), BF), pltpu.VMEM((2, WIDE, 512), F32)],
        flops=2 * 2**30,
        nbytes=6 * 2**20,
    )(flags, modin, modin_other, second_w, *far)
    third_w = gather_z(after(third_w, packed))
    packed = lax.all_to_all(packed, ("xh", "y"), 0, 0, tiled=True)
    attn = spatial_attend(packed)
    w0_out = third_w[:, :HALF], third_w[:, LAST : LAST + HALF]
    w0_partner = tuple(core_swap(w) for w in w0_out)
    attn = lax.all_to_all(attn, ("xh", "y"), 0, 0, tiled=True).reshape(HALF, 512)
    a_rec = core_swap(attn[:, TOK:])
    block_out, ns = call(
        last_kernel,
        "last",
        (sds(TOK, D), sds(TOK, D)),
        [SMEM] + [VMEM] * 9,
        flops=2**30,
        nbytes=6 * 2**20,
    )(flags, attn, a_rec, *w0_out, *w0_partner, h2, nt, mods)
    whole = (2, 1, 128, D)
    return block_out.reshape(whole), ns.reshape(whole), nt.reshape(whole)


def solution(mesh):
    fine = Mesh(mesh.devices.reshape(2, 8, 2, 4, 2), ("xl", "z", "xh", "y", "c"))
    tokens = P(None, TM, SPACE, None)
    return jax.shard_map(
        shards,
        mesh=fine,
        in_specs=(tokens, tokens, P(), P(None, TM, None)),
        out_specs=(tokens, tokens, tokens),
        check_vma=False,
    )
```
